32 devices in a mesh: img: 4 (over z), gx: 2 (over x), gz: 4 (over y, core).
Axes of the slice: x: 2, y: 2, z: 4, core: 2. Of those that a mesh axis runs over, the one named last changes fastest.
Arguments:
- species: float32 [4, 2, 32, 16, 512], P('img', None, 'gx', None, 'gz'), may hold values from -2.5 to 2.5
- diffusion: float32 [2, 32, 16, 512], P(None, 'gx', None, 'gz'), may hold values from 0.1 to 2
- z_inverse: float32 [2, 512, 512], replicated, may hold values from -1 to 1.5
- starts: int32 [4], replicated, may hold values from -1 to 1, as said below
- weights: float32 [4, 4], replicated, may hold values from -0.1 to 1, as said below
Outputs:
- new_string: float32 [4, 2, 32, 16, 512], P('img', None, 'gx', None, 'gz')
The draws below stay inside these ranges and needn't reach their ends.
Inputs may be any that keep to these rules, and one draw needn't show every extreme that they name: starts[t] is t - 2 or t - 1. Each row holds the cubic Lagrange weights at a point between the second and third of four equally spaced images.
All inputs are finite; a program needn't handle non-finite values.
Results may differ from the reference program's by a relative error of at most 0.00012.
Values sent between devices are 32-bit elements; how exact they have to be, the bound alone decides.
A program may use at most 64 MiB of HBM per device.

```python
import math
import jax
import jax.numpy as jnp
from jax import lax

NY = 16
STEPS = 4
IMAGES = 4
NX = 32
NZ = 512


def draw_z_inverse(key, part):
    first_key, second_key = jax.random.split(jax.random.fold_in(key, 7))
    theta = jnp.exp(jax.random.uniform(first_key, (2, 1, 1), jnp.float32, jnp.log(0.5 / NZ), jnp.log(2.0 / NZ)))
    places = jnp.arange(NZ, dtype=jnp.float32)
    distance = jnp.abs(places[:, None] - places[None, :])
    decay = jnp.exp(-theta)
    smooth = jnp.exp(-theta * distance) * (1.0 - decay) / (1.0 + decay)
    noise = jnp.clip(jax.random.normal(second_key, (2, NZ, NZ), jnp.float32), -4.0, 4.0)
    identity = (distance == 0.0).astype(jnp.float32)
    return 0.6 * identity + 0.4 * smooth + 0.3 * noise / jnp.sqrt(NZ * 1.0)


def draw_starts(key, part):
    target = jnp.arange(IMAGES, dtype=jnp.int32)
    choice_bits = jax.random.randint(jax.random.fold_in(key, 11), (IMAGES,), 0, 2, jnp.int32)
    random_place = (target == 1) | (target > IMAGES // 2) & (target < IMAGES - 1)
    late = ((target == IMAGES - 1) | (target == 2)).astype(jnp.int32)
    extra = jnp.where(random_place, choice_bits, late)
    return target - 1 - extra


def draw_weights(key, part):
    frac = jax.random.uniform(jax.random.fold_in(key, 13), (IMAGES,), jnp.float32, 0.2, 0.8)
    point = 1.0 + frac
    first = -(point - 1.0) * (point - 2.0) * (point - 3.0) / 6.0
    second = point * (point - 2.0) * (point - 3.0) / 2.0
    third = -point * (point - 1.0) * (point - 3.0) / 2.0
    fourth = point * (point - 1.0) * (point - 2.0) / 6.0
    return jnp.stack([first, second, third, fourth], axis=1)


def block_scale(rng, shape, cuts, least, largest):
    gain, own = 1.0, jax.random.fold_in(rng, 6)
    for dim, parts in cuts:
        heights = jnp.exp(jax.random.uniform(jax.random.fold_in(own, dim), (parts,), jnp.float32, least / len(cuts), largest / len(cuts)))
        gain = gain * jnp.repeat(heights, shape[dim] // parts).reshape([-1 if axis == dim else 1 for axis in range(len(shape))])
    return gain


def centred(rng, dims, scale, most, pieces=(), kind=jnp.bfloat16):
    values = jax.random.normal(rng, dims, jnp.float32) * scale
    if len(pieces) > 0:
        values = block_scale(rng, dims, pieces, -0.22, 0.18) * values
    return jnp.clip(values, min=-most, max=most).astype(kind)


def setup_inputs(seed: int = 0) -> dict:
    keys = jax.random.split(jax.random.key(seed), 6)
    return {
        "species": centred(keys[0], (IMAGES, 2, NX, NY, NZ), 0.8, 2.5, ((0, 4), (2, 2), (4, 4)), jnp.float32),
        "diffusion": jnp.clip(jnp.exp(math.log(2.0) - 2.9957323 * jax.random.uniform(keys[1], (2, NX, NY, NZ), jnp.float32) ** block_scale(keys[1], (2, NX, NY, NZ), ((1, 2), (3, 4)), -0.2, 0.2)), 0.1, 2.0),
        "z_inverse": draw_z_inverse(jax.random.fold_in(keys[5], 71), 0),
        "starts": draw_starts(jax.random.fold_in(keys[5], 71), 0),
        "weights": draw_weights(jax.random.fold_in(keys[5], 71), 0),
    }


step_size = 0.05


def reaction(state):
    first = state[0]
    second = state[1]
    return jnp.stack([first - first * first * first - second + 0.2, 0.5 * (first - second)])


def spread_flux(state, padded, coeffs):
    centre = coeffs[:, 1:-1, 1:-1]
    total = (centre + coeffs[:, :-2, 1:-1]) * (padded[:, :-2, 1:-1] - state)
    total = total + (centre + coeffs[:, 2:, 1:-1]) * (padded[:, 2:, 1:-1] - state)
    total = total + (centre + coeffs[:, 1:-1, :-2]) * (padded[:, 1:-1, :-2] - state)
    total = total + (centre + coeffs[:, 1:-1, 2:]) * (padded[:, 1:-1, 2:] - state)
    return 0.5 * total


def reference(species, diffusion, z_inverse, starts, weights):
    widths = ((0, 0), (1, 1), (1, 1), (0, 0))
    coeffs = jnp.pad(diffusion, widths)

    def evolve(state):
        for repeat in range(STEPS):
            padded = jnp.pad(state, widths)
            source = state + step_size * (reaction(state) + spread_flux(state, padded, coeffs))
            state = jnp.einsum("sij,sabj->sabi", z_inverse, source, precision=lax.Precision.HIGHEST)
        return state

    evolved = lax.map(evolve, species)
    images = species.shape[0]
    target = jnp.arange(images, dtype=jnp.int32)
    stacked = jnp.pad(evolved, ((2, 2), (0, 0), (0, 0), (0, 0), (0, 0)))
    result = None
    for offset in range(-2, 3):
        coef = jnp.zeros((images,), jnp.float32)
        for place in range(4):
            coef = coef + jnp.where(starts + place == target + offset, weights[:, place], 0.0)
        term = coef[:, None, None, None, None] * stacked[2 + offset:2 + offset + images]
        result = term if result is None else result + term
    return result
```

```python
import functools

import jax
import jax.numpy as jnp
from jax import lax
from jax.experimental import pallas as pl
from jax.experimental.pallas import tpu as pltpu
from jax.sharding import PartitionSpec as P

STEPS = 4
HALO = 1


step_size = 0.05
MESH = pl.DeviceIdType.MESH
both = (0, 1)


def kernel(
    sizes,
    species_ref,
    diffusion_ref,
    z_ref,
    starts_ref,
    weights_ref,
    out_ref,
    z_raw,
    z_high,
    z_low,
    coeffs,
    states,
    lhs,
    evolved,
    near,
    far,
    result,
    local_sem,
    swap_send,
    swap_recv,
    edge_send,
    edge_recv,
    row_send,
    row_recv,
    near_send,
    near_recv,
    far_send,
    far_recv,
    back_send,
    back_recv,
):
    images, nx, nz, width, ny, lanes = sizes
    rows = width // nz
    image, gx, gz = lax.axis_index("img"), lax.axis_index("gx"), lax.axis_index("gz")
    strip = gx * nz + gz
    strips = nx * nz
    full = rows + 2 * HALO

    load_z = pltpu.make_async_copy(z_ref, z_raw, local_sem.at[0])
    load_z.start()

    barrier = pltpu.get_barrier_semaphore()
    for step in range(1, nz):
        other = lax.rem(gz + step, nz)
        pl.semaphore_signal(barrier, inc=1, device_id={"gz": other}, device_id_type=MESH)

    def greet(condition, where):
        @pl.when(condition)
        def _():
            pl.semaphore_signal(barrier, inc=1, device_id=where, device_id_type=MESH)

    greet(image > 0, {"img": image - 1})
    greet(image < images - 1, {"img": image + 1})
    greet(gx > 0, {"gx": gx - 1, "gz": nz - 1})
    greet(gx < nx - 1, {"gx": gx + 1, "gz": 0})

    @pl.when(gz == 0)
    def _():
        for other in range(nz):
            greet(gx > 0, {"gx": gx - 1, "gz": other})

    @pl.when(gz == nz - 1)
    def _():
        for other in range(nz):
            greet(gx < nx - 1, {"gx": gx + 1, "gz": other})

    def one(condition):
        return jnp.where(condition, 1, 0)

    below, above = one(gx > 0), one(gx < nx - 1)
    expected = (nz - 1) + one(image > 0) + one(image < images - 1) + below + above
    expected = expected + nz * (below * one(gz == 0) + above * one(gz == nz - 1))
    pl.semaphore_wait(barrier, expected)

    sources = (diffusion_ref, species_ref.at[0])
    targets = (coeffs, states.at[0])

    def span(k):
        return max(0, k * rows - HALO), min(width, k * rows + rows + HALO)

    def swap(which, k, sender):
        low, high = span(k)
        first = low - (k * rows - HALO)
        return pltpu.make_async_remote_copy(
            src_ref=sources[which].at[:, low:high],
            dst_ref=targets[which].at[:, sender, first : first + high - low],
            send_sem=swap_send.at[which, k],
            recv_sem=swap_recv.at[which, sender],
            device_id={"gz": k},
            device_id_type=MESH,
        )

    def own(which, k):
        low, high = span(k)
        first = low - (k * rows - HALO)
        return pltpu.make_async_copy(
            sources[which].at[:, low:high],
            targets[which].at[:, k, first : first + high - low],
            local_sem.at[1 + which],
        )

    def edge_up(which, sender):
        return pltpu.make_async_remote_copy(
            src_ref=sources[which].at[:, width - HALO : width],
            dst_ref=targets[which].at[:, sender, 0:HALO],
            send_sem=edge_send.at[which, 0],
            recv_sem=edge_recv.at[which, 0, sender],
            device_id={"gx": gx + 1, "gz": 0},
            device_id_type=MESH,
        )

    def edge_down(which, sender):
        return pltpu.make_async_remote_copy(
            src_ref=sources[which].at[:, 0:HALO],
            dst_ref=targets[which].at[:, sender, rows + HALO : full],
            send_sem=edge_send.at[which, 1],
            recv_sem=edge_recv.at[which, 1, sender],
            device_id={"gx": gx - 1, "gz": nz - 1},
            device_id_type=MESH,
        )

    for which in (1, 0):
        for me in range(nz):

            @pl.when(gz == me)
            def _(which=which, me=me):
                for step in range(1, nz):
                    swap(which, (me + step) % nz, me).start()
                own(which, me).start()

        @pl.when(gx < nx - 1)
        def _(which=which):
            edge_up(which, gz).start()

        @pl.when(gx > 0)
        def _(which=which):
            edge_down(which, gz).start()

    @pl.when(strip == 0)
    def _():
        for part in (coeffs, *[states.at[i] for i in range(STEPS)]):
            part[:, :, 0:HALO] = jnp.zeros((2, nz, HALO, ny, lanes), jnp.float32)

    @pl.when(strip == strips - 1)
    def _():
        for part in (coeffs, *[states.at[i] for i in range(STEPS)]):
            part[:, :, rows + HALO : full] = jnp.zeros((2, nz, HALO, ny, lanes), jnp.float32)

    def clear(condition, part):
        @pl.when(condition)
        def _():
            part[...] = jnp.zeros(part.shape, jnp.float32)

    clear(image < 1, near.at[0])
    clear(image > images - 2, near.at[1])
    clear(image < 2, far.at[0])
    clear(image > images - 3, far.at[1])

    load_z.wait()
    for s in both:
        for block in range(nz):
            part = slice(block * lanes, (block + 1) * lanes)
            turned = z_raw[s, part, :].T
            high = turned.astype(jnp.bfloat16)
            z_high[s, :, part] = high
            z_low[s, :, part] = (turned - high.astype(jnp.float32)).astype(jnp.bfloat16)

    def arrived(which):
        for me in range(nz):

            @pl.when(gz == me)
            def _(me=me):
                own(which, me).wait()
                for sender in range(nz):
                    if sender != me:
                        low, high = span(me)
                        first = low - (me * rows - HALO)
                        part = targets[which].at[:, sender, first : first + high - low]
                        pltpu.make_async_copy(part, part, swap_recv.at[which, sender]).wait()

        @pl.when((gz == 0) & (gx > 0))
        def _():
            for sender in range(nz):
                edge_up(which, sender).wait_recv()

        @pl.when((gz == nz - 1) & (gx < nx - 1))
        def _():
            for sender in range(nz):
                edge_down(which, sender).wait_recv()

    def row_up(step, s):
        p = strip + 1
        return pltpu.make_async_remote_copy(
            src_ref=states.at[step, s, :, rows],
            dst_ref=states.at[step, s, :, 0],
            send_sem=row_send.at[step, s, 0],
            recv_sem=row_recv.at[step, s, 0],
            device_id={"gx": lax.div(p, nz), "gz": lax.rem(p, nz)},
            device_id_type=MESH,
        )

    def row_down(step, s):
        p = strip - 1 + nz
        return pltpu.make_async_remote_copy(
            src_ref=states.at[step, s, :, 1],
            dst_ref=states.at[step, s, :, rows + 1],
            send_sem=row_send.at[step, s, 1],
            recv_sem=row_recv.at[step, s, 1],
            device_id={"gx": lax.div(p, nz) - 1, "gz": lax.rem(p, nz)},
            device_id_type=MESH,
        )

    place = lax.broadcasted_iota(jnp.int32, (rows, ny, lanes), 1)
    arrived(1)
    arrived(0)
    half = 0.5 * step_size
    cells = rows * ny

    def to_near(s, g, side):
        return pltpu.make_async_remote_copy(
            src_ref=evolved.at[s, g],
            dst_ref=near.at[side, s, g],
            send_sem=near_send.at[side, s, g],
            recv_sem=near_recv.at[side, s, g],
            device_id={"img": image + 1 - 2 * side},
            device_id_type=MESH,
        )

    def to_far(s, g, side):
        return pltpu.make_async_remote_copy(
            src_ref=near.at[side, s, g],
            dst_ref=far.at[side, s, g],
            send_sem=far_send.at[side, s, g],
            recv_sem=far_recv.at[side, s, g],
            device_id={"img": image + 1 - 2 * side},
            device_id_type=MESH,
        )

    can_send = (image < images - 1, image > 0)
    has_near = (image > 0, image < images - 1)
    has_far = (image > 1, image < images - 2)

    for step in range(STEPS):
        state = states.at[step]
        if step > 0:
            for s in both:

                @pl.when(strip > 0)
                def _(s=s):
                    row_up(step, s).wait_recv()

                @pl.when(strip < strips - 1)
                def _(s=s):
                    row_down(step, s).wait_recv()

        for g in range(nz):
            first, second = state[0, g, 1 : rows + 1], state[1, g, 1 : rows + 1]
            reactions = (
                first - first * first * first - second + 0.2,
                0.5 * (first - second),
            )
            for s in both:
                c = state[s, g]
                d = coeffs[s, g]
                across = (d[:-1] + d[1:]) * (c[1:] - c[:-1])
                centre, spread = c[1:-1], d[1:-1]
                last = place == ny - 1
                c_next = jnp.where(last, 0.0, pltpu.roll(centre, ny - 1, 1))
                d_next = jnp.where(last, 0.0, pltpu.roll(spread, ny - 1, 1))
                along = (spread + d_next) * (c_next - centre)
                before = jnp.where(place == 0, spread * centre, pltpu.roll(along, 1, 1))
                flux = (across[1:] - across[:-1]) + (along - before)
                source = centre + step_size * reactions[s] + half * flux
                source = source.reshape(cells, lanes)
                high = source.astype(jnp.bfloat16)
                part = slice(g * lanes, (g + 1) * lanes)
                lhs[s, 0:cells, part] = high
                lhs[s, cells : 2 * cells, part] = (source - high.astype(jnp.float32)).astype(jnp.bfloat16)

        for s in both:
            product = jnp.dot(lhs[s], z_high[s], preferred_element_type=jnp.float32)
            small = jnp.dot(lhs[s, 0:cells], z_low[s], preferred_element_type=jnp.float32)
            solved = product[0:cells] + (product[cells : 2 * cells] + small)
            for g in range(nz):
                block = solved[:, g * lanes : (g + 1) * lanes].reshape(rows, ny, lanes)
                if step < STEPS - 1:
                    states[step + 1, s, g, 1 : rows + 1] = block
                else:
                    evolved[s, g] = block
            if step < STEPS - 1:

                @pl.when(strip < strips - 1)
                def _(s=s, step=step):
                    row_up(step + 1, s).start()

                @pl.when(strip > 0)
                def _(s=s, step=step):
                    row_down(step + 1, s).start()

            else:
                for g in range(nz):
                    for side in both:

                        @pl.when(can_send[side])
                        def _(s=s, g=g, side=side):
                            to_near(s, g, side).start()

    for s in both:
        for g in range(nz):
            for side in both:

                @pl.when(has_near[side])
                def _(s=s, g=g, side=side):
                    to_near(s, g, side).wait_recv()

                    @pl.when(can_send[side])
                    def _():
                        to_far(s, g, side).start()

    start = starts_ref[image]

    def coef(offset):
        total = jnp.float32(0.0)
        for k in range(4):
            total = total + jnp.where(start + k == image + offset, weights_ref[image, k], 0.0)
        return total

    coefs = [coef(offset) for offset in range(-2, 3)]

    def back(s, g, sender):
        return pltpu.make_async_remote_copy(
            src_ref=result.at[s, g],
            dst_ref=out_ref.at[0, s, pl.ds(sender * rows, rows)],
            send_sem=back_send.at[s, g],
            recv_sem=back_recv.at[s, sender],
            device_id={"gz": g},
            device_id_type=MESH,
        )

    def keep(s, g):
        return pltpu.make_async_copy(
            result.at[s, g], out_ref.at[0, s, pl.ds(gz * rows, rows)], back_send.at[s, g]
        )

    for s in both:
        for g in range(nz):
            for side in both:

                @pl.when(has_far[side])
                def _(s=s, g=g, side=side):
                    to_far(s, g, side).wait_recv()

            total = coefs[0] * far[0, s, g] + coefs[1] * near[0, s, g]
            total = total + coefs[2] * evolved[s, g]
            total = total + coefs[3] * near[1, s, g] + coefs[4] * far[1, s, g]
            result[s, g] = total

            @pl.when(gz != g)
            def _(s=s, g=g):
                back(s, g, gz).start()

            @pl.when(gz == g)
            def _(s=s, g=g):
                keep(s, g).start()

    for which in both:
        for k in range(nz):

            @pl.when(gz != k)
            def _(which=which, k=k):
                swap(which, k, gz).wait_send()

        @pl.when(gx < nx - 1)
        def _(which=which):
            edge_up(which, gz).wait_send()

        @pl.when(gx > 0)
        def _(which=which):
            edge_down(which, gz).wait_send()

    for step in range(1, STEPS):
        for s in both:

            @pl.when(strip < strips - 1)
            def _(s=s, step=step):
                row_up(step, s).wait_send()

            @pl.when(strip > 0)
            def _(s=s, step=step):
                row_down(step, s).wait_send()

    for s in both:
        for g in range(nz):
            for side in both:

                @pl.when(can_send[side])
                def _(s=s, g=g, side=side):
                    to_near(s, g, side).wait_send()

                @pl.when(can_send[side] & has_near[side])
                def _(s=s, g=g, side=side):
                    to_far(s, g, side).wait_send()

            @pl.when(gz != g)
            def _(s=s, g=g):
                back(s, g, gz).wait_send()
                back(s, g, g).wait_recv()

            @pl.when(gz == g)
            def _(s=s, g=g):
                keep(s, g).wait()


def local(sizes, species, diffusion, z_inverse, starts, weights):
    images, nx, nz, width, ny, lanes = sizes
    rows = width // nz
    depth = nz * lanes
    full = rows + 2 * HALO
    dma = pltpu.SemaphoreType.DMA
    anywhere = pl.BlockSpec(memory_space=pl.ANY)
    scalars = pl.BlockSpec(memory_space=pltpu.SMEM)
    lines = (2, nz, rows, ny, lanes)
    return pl.pallas_call(
        functools.partial(kernel, sizes),
        out_shape=jax.ShapeDtypeStruct(species.shape, jnp.float32),
        in_specs=[anywhere, anywhere, anywhere, scalars, scalars],
        out_specs=anywhere,
        scratch_shapes=[
            pltpu.VMEM((2, depth, depth), jnp.float32),
            pltpu.VMEM((2, depth, depth), jnp.bfloat16),
            pltpu.VMEM((2, depth, depth), jnp.bfloat16),
            pltpu.VMEM((2, nz, full, ny, lanes), jnp.float32),
            pltpu.VMEM((STEPS, 2, nz, full, ny, lanes), jnp.float32),
            pltpu.VMEM((2, 2 * rows * ny, depth), jnp.bfloat16),
            pltpu.VMEM(lines, jnp.float32),
            pltpu.VMEM((2, *lines), jnp.float32),
            pltpu.VMEM((2, *lines), jnp.float32),
            pltpu.VMEM(lines, jnp.float32),
            dma((3,)),
            dma((2, nz)),
            dma((2, nz)),
            dma((2, 2)),
            dma((2, 2, nz)),
            dma((STEPS, 2, 2)),
            dma((STEPS, 2, 2)),
            dma((2, 2, nz)),
            dma((2, 2, nz)),
            dma((2, 2, nz)),
            dma((2, 2, nz)),
            dma((2, nz)),
            dma((2, nz)),
        ],
        compiler_params=pltpu.CompilerParams(
            collective_id=0, has_side_effects=True, vmem_limit_bytes=48 * 1024 * 1024
        ),
    )(species, diffusion, z_inverse, starts, weights)


def solution(mesh):
    images, nx, nz = (mesh.shape[axis] for axis in ("img", "gx", "gz"))

    def body(species, diffusion, z_inverse, starts, weights):
        sizes = (images, nx, nz, *species.shape[2:])
        return local(sizes, species, diffusion, z_inverse, starts, weights)

    return jax.shard_map(
        body,
        mesh=mesh,
        in_specs=(P("img", None, "gx", None, "gz"), P(None, "gx", None, "gz"), P(), P(), P()),
        out_specs=P("img", None, "gx", None, "gz"),
        check_vma=False,
    )
```

```python
import functools

import jax
import jax.numpy as jnp
from jax import lax
from jax.experimental import pallas as pl
from jax.experimental.pallas import tpu as pltpu
from jax.sharding import PartitionSpec as P

STEPS = 4
HALO = 2


step_size = 0.05
MESH = pl.DeviceIdType.MESH
both = (0, 1)


def kernel(
    sizes,
    species_ref,
    diffusion_ref,
    z_ref,
    starts_hbm,
    weights_hbm,
    out_ref,
    z_raw,
    z_high,
    z_low,
    coeffs,
    states,
    lhs,
    evolved,
    near,
    far,
    result,
    starts_ref,
    weights_ref,
    local_sem,
    swap_send,
    swap_recv,
    edge_send,
    edge_recv,
    row_send,
    row_recv,
    near_send,
    near_recv,
    far_send,
    far_recv,
    back_send,
    back_recv,
):
    images, nx, nz, width, ny, lanes = sizes
    rows = width // nz
    image, gx, gz = lax.axis_index("img"), lax.axis_index("gx"), lax.axis_index("gz")
    strip = gx * nz + gz
    strips = nx * nz
    full = rows + 2 * HALO
    trades = tuple(step for step in range(1, STEPS) if step % HALO == 0)

    load_z = pltpu.make_async_copy(z_ref, z_raw, local_sem.at[0])
    load_z.start()
    load_starts = pltpu.make_async_copy(starts_hbm, starts_ref, local_sem.at[3])
    load_starts.start()
    load_weights = pltpu.make_async_copy(weights_hbm, weights_ref, local_sem.at[4])
    load_weights.start()

    barrier = pltpu.get_barrier_semaphore()
    for step in range(1, nz):
        other = lax.rem(gz + step, nz)
        pl.semaphore_signal(barrier, inc=1, device_id={"gz": other}, device_id_type=MESH)

    def greet(condition, where):
        @pl.when(condition)
        def _():
            pl.semaphore_signal(barrier, inc=1, device_id=where, device_id_type=MESH)

    greet(image > 0, {"img": image - 1})
    greet(image < images - 1, {"img": image + 1})
    greet(gx > 0, {"gx": gx - 1, "gz": nz - 1})
    greet(gx < nx - 1, {"gx": gx + 1, "gz": 0})

    @pl.when(gz == 0)
    def _():
        for other in range(nz):
            greet(gx > 0, {"gx": gx - 1, "gz": other})

    @pl.when(gz == nz - 1)
    def _():
        for other in range(nz):
            greet(gx < nx - 1, {"gx": gx + 1, "gz": other})

    def one(condition):
        return jnp.where(condition, 1, 0)

    below, above = one(gx > 0), one(gx < nx - 1)
    expected = (nz - 1) + one(image > 0) + one(image < images - 1) + below + above
    expected = expected + nz * (below * one(gz == 0) + above * one(gz == nz - 1))
    pl.semaphore_wait(barrier, expected)

    sources = (diffusion_ref, species_ref.at[0])
    targets = (coeffs, states.at[0])

    def span(k):
        return max(0, k * rows - HALO), min(width, k * rows + rows + HALO)

    def swap(which, k, sender):
        low, high = span(k)
        first = low - (k * rows - HALO)
        return pltpu.make_async_remote_copy(
            src_ref=sources[which].at[:, low:high],
            dst_ref=targets[which].at[:, sender, first : first + high - low],
            send_sem=swap_send.at[which, k],
            recv_sem=swap_recv.at[which, sender],
            device_id={"gz": k},
            device_id_type=MESH,
        )

    def own(which, k):
        low, high = span(k)
        first = low - (k * rows - HALO)
        return pltpu.make_async_copy(
            sources[which].at[:, low:high],
            targets[which].at[:, k, first : first + high - low],
            local_sem.at[1 + which],
        )

    def edge_up(which, sender):
        return pltpu.make_async_remote_copy(
            src_ref=sources[which].at[:, width - HALO : width],
            dst_ref=targets[which].at[:, sender, 0:HALO],
            send_sem=edge_send.at[which, 0],
            recv_sem=edge_recv.at[which, 0, sender],
            device_id={"gx": gx + 1, "gz": 0},
            device_id_type=MESH,
        )

    def edge_down(which, sender):
        return pltpu.make_async_remote_copy(
            src_ref=sources[which].at[:, 0:HALO],
            dst_ref=targets[which].at[:, sender, rows + HALO : full],
            send_sem=edge_send.at[which, 1],
            recv_sem=edge_recv.at[which, 1, sender],
            device_id={"gx": gx - 1, "gz": nz - 1},
            device_id_type=MESH,
        )

    for which in (1, 0):
        for me in range(nz):

            @pl.when(gz == me)
            def _(which=which, me=me):
                for step in range(1, nz):
                    swap(which, (me + step) % nz, me).start()
                own(which, me).start()

        @pl.when(gx < nx - 1)
        def _(which=which):
            edge_up(which, gz).start()

        @pl.when(gx > 0)
        def _(which=which):
            edge_down(which, gz).start()

    @pl.when(strip == 0)
    def _():
        for part in (coeffs, *[states.at[i] for i in (0, *trades)]):
            part[:, :, 0:HALO] = jnp.zeros((2, nz, HALO, ny, lanes), jnp.float32)

    @pl.when(strip == strips - 1)
    def _():
        for part in (coeffs, *[states.at[i] for i in (0, *trades)]):
            part[:, :, rows + HALO : full] = jnp.zeros((2, nz, HALO, ny, lanes), jnp.float32)

    def clear(condition, part):
        @pl.when(condition)
        def _():
            part[...] = jnp.zeros(part.shape, jnp.float32)

    clear(image < 1, near.at[0])
    clear(image > images - 2, near.at[1])
    clear(image < 2, far.at[0])
    clear(image > images - 3, far.at[1])

    load_z.wait()
    for s in both:
        for block in range(nz):
            part = slice(block * lanes, (block + 1) * lanes)
            turned = z_raw[s, part, :].T
            high = turned.astype(jnp.bfloat16)
            z_high[s, :, part] = high
            z_low[s, :, part] = (turned - high.astype(jnp.float32)).astype(jnp.bfloat16)

    def arrived(which):
        for me in range(nz):

            @pl.when(gz == me)
            def _(me=me):
                own(which, me).wait()
                for sender in range(nz):
                    if sender != me:
                        low, high = span(me)
                        first = low - (me * rows - HALO)
                        part = targets[which].at[:, sender, first : first + high - low]
                        pltpu.make_async_copy(part, part, swap_recv.at[which, sender]).wait()

        @pl.when((gz == 0) & (gx > 0))
        def _():
            for sender in range(nz):
                edge_up(which, sender).wait_recv()

        @pl.when((gz == nz - 1) & (gx < nx - 1))
        def _():
            for sender in range(nz):
                edge_down(which, sender).wait_recv()

    def row_up(step, s):
        p = strip + 1
        return pltpu.make_async_remote_copy(
            src_ref=states.at[step, s, :, rows : rows + HALO],
            dst_ref=states.at[step, s, :, 0:HALO],
            send_sem=row_send.at[step, s, 0],
            recv_sem=row_recv.at[step, s, 0],
            device_id={"gx": lax.div(p, nz), "gz": lax.rem(p, nz)},
            device_id_type=MESH,
        )

    def row_down(step, s):
        p = strip - 1 + nz
        return pltpu.make_async_remote_copy(
            src_ref=states.at[step, s, :, HALO : 2 * HALO],
            dst_ref=states.at[step, s, :, rows + HALO : full],
            send_sem=row_send.at[step, s, 1],
            recv_sem=row_recv.at[step, s, 1],
            device_id={"gx": lax.div(p, nz) - 1, "gz": lax.rem(p, nz)},
            device_id_type=MESH,
        )

    arrived(1)
    arrived(0)
    half = 0.5 * step_size

    def to_near(s, g, side):
        return pltpu.make_async_remote_copy(
            src_ref=evolved.at[s, g],
            dst_ref=near.at[side, s, g],
            send_sem=near_send.at[side, s, g],
            recv_sem=near_recv.at[side, s, g],
            device_id={"img": image + 1 - 2 * side},
            device_id_type=MESH,
        )

    def to_far(s, g, side):
        return pltpu.make_async_remote_copy(
            src_ref=near.at[side, s, g],
            dst_ref=far.at[side, s, g],
            send_sem=far_send.at[side, s, g],
            recv_sem=far_recv.at[side, s, g],
            device_id={"img": image + 1 - 2 * side},
            device_id_type=MESH,
        )

    can_send = (image < images - 1, image > 0)
    has_near = (image > 0, image < images - 1)
    has_far = (image > 1, image < images - 2)

    for step in range(STEPS):
        state = states.at[step]
        if step in trades:
            for s in both:

                @pl.when(strip > 0)
                def _(s=s):
                    row_up(step, s).wait_recv()

                @pl.when(strip < strips - 1)
                def _(s=s):
                    row_down(step, s).wait_recv()

        spare = HALO - 1 - step % HALO
        if step == STEPS - 1:
            spare = 0
        count = rows + 2 * spare
        low, cells = HALO - spare, count * ny
        inner = slice(low, low + count)
        outer = slice(low - 1, low + count + 1)
        place = lax.broadcasted_iota(jnp.int32, (count, ny, lanes), 1)
        row = lax.broadcasted_iota(jnp.int32, (count, ny, lanes), 0)
        beyond = (strip == 0) & (row < spare) | (strip == strips - 1) & (row >= rows + spare)
        for g in range(nz):
            first, second = state[0, g, inner], state[1, g, inner]
            reactions = (
                first - first * first * first - second + 0.2,
                0.5 * (first - second),
            )
            for s in both:
                c = state[s, g, outer]
                d = coeffs[s, g, outer]
                across = (d[:-1] + d[1:]) * (c[1:] - c[:-1])
                centre, spread = c[1:-1], d[1:-1]
                last = place == ny - 1
                c_next = jnp.where(last, 0.0, pltpu.roll(centre, ny - 1, 1))
                d_next = jnp.where(last, 0.0, pltpu.roll(spread, ny - 1, 1))
                along = (spread + d_next) * (c_next - centre)
                before = jnp.where(place == 0, spread * centre, pltpu.roll(along, 1, 1))
                flux = (across[1:] - across[:-1]) + (along - before)
                source = centre + step_size * reactions[s] + half * flux
                if spare > 0:
                    source = jnp.where(beyond, 0.0, source)
                source = source.reshape(cells, lanes)
                high = source.astype(jnp.bfloat16)
                part = slice(g * lanes, (g + 1) * lanes)
                lhs[s, 0:cells, part] = high
                lhs[s, cells : 2 * cells, part] = (source - high.astype(jnp.float32)).astype(jnp.bfloat16)

        for s in both:
            product = jnp.dot(lhs[s], z_high[s], preferred_element_type=jnp.float32)
            small = jnp.dot(lhs[s, 0:cells], z_low[s], preferred_element_type=jnp.float32)
            solved = product[0:cells] + (product[cells : 2 * cells] + small)
            for g in range(nz):
                block = solved[:, g * lanes : (g + 1) * lanes].reshape(count, ny, lanes)
                if step < STEPS - 1:
                    states[step + 1, s, g, inner] = block
                else:
                    evolved[s, g] = block
            if step + 1 in trades:

                @pl.when(strip < strips - 1)
                def _(s=s, step=step):
                    row_up(step + 1, s).start()

                @pl.when(strip > 0)
                def _(s=s, step=step):
                    row_down(step + 1, s).start()

            elif step == STEPS - 1:
                for g in range(nz):
                    for side in both:

                        @pl.when(can_send[side])
                        def _(s=s, g=g, side=side):
                            to_near(s, g, side).start()

    for s in both:
        for g in range(nz):
            for side in both:

                @pl.when(has_near[side])
                def _(s=s, g=g, side=side):
                    to_near(s, g, side).wait_recv()

                    @pl.when(can_send[side])
                    def _():
                        to_far(s, g, side).start()

    load_starts.wait()
    load_weights.wait()
    start = starts_ref[image]

    def coef(offset):
        total = jnp.float32(0.0)
        for k in range(4):
            total = total + jnp.where(start + k == image + offset, weights_ref[image, k], 0.0)
        return total

    coefs = [coef(offset) for offset in range(-2, 3)]

    def back(s, g, sender):
        return pltpu.make_async_remote_copy(
            src_ref=result.at[s, g],
            dst_ref=out_ref.at[0, s, pl.ds(sender * rows, rows)],
            send_sem=back_send.at[s, g],
            recv_sem=back_recv.at[s, sender],
            device_id={"gz": g},
            device_id_type=MESH,
        )

    def keep(s, g):
        return pltpu.make_async_copy(
            result.at[s, g], out_ref.at[0, s, pl.ds(gz * rows, rows)], back_send.at[s, g]
        )

    for s in both:
        for g in range(nz):
            for side in both:

                @pl.when(has_far[side])
                def _(s=s, g=g, side=side):
                    to_far(s, g, side).wait_recv()

            total = coefs[0] * far[0, s, g] + coefs[1] * near[0, s, g]
            total = total + coefs[2] * evolved[s, g]
            total = total + coefs[3] * near[1, s, g] + coefs[4] * far[1, s, g]
            result[s, g] = total

            @pl.when(gz != g)
            def _(s=s, g=g):
                back(s, g, gz).start()

            @pl.when(gz == g)
            def _(s=s, g=g):
                keep(s, g).start()

    for which in both:
        for k in range(nz):

            @pl.when(gz != k)
            def _(which=which, k=k):
                swap(which, k, gz).wait_send()

        @pl.when(gx < nx - 1)
        def _(which=which):
            edge_up(which, gz).wait_send()

        @pl.when(gx > 0)
        def _(which=which):
            edge_down(which, gz).wait_send()

    for step in trades:
        for s in both:

            @pl.when(strip < strips - 1)
            def _(s=s, step=step):
                row_up(step, s).wait_send()

            @pl.when(strip > 0)
            def _(s=s, step=step):
                row_down(step, s).wait_send()

    for s in both:
        for g in range(nz):
            for side in both:

                @pl.when(can_send[side])
                def _(s=s, g=g, side=side):
                    to_near(s, g, side).wait_send()

                @pl.when(can_send[side] & has_near[side])
                def _(s=s, g=g, side=side):
                    to_far(s, g, side).wait_send()

            @pl.when(gz != g)
            def _(s=s, g=g):
                back(s, g, gz).wait_send()
                back(s, g, g).wait_recv()

            @pl.when(gz == g)
            def _(s=s, g=g):
                keep(s, g).wait()


def local(sizes, species, diffusion, z_inverse, starts, weights):
    images, nx, nz, width, ny, lanes = sizes
    rows = width // nz
    depth = nz * lanes
    full = rows + 2 * HALO
    dma = pltpu.SemaphoreType.DMA
    anywhere = pl.BlockSpec(memory_space=pl.ANY)
    lines = (2, nz, rows, ny, lanes)
    return pl.pallas_call(
        functools.partial(kernel, sizes),
        out_shape=jax.ShapeDtypeStruct(species.shape, jnp.float32),
        in_specs=[anywhere] * 5,
        out_specs=anywhere,
        scratch_shapes=[
            pltpu.VMEM((2, depth, depth), jnp.float32),
            pltpu.VMEM((2, depth, depth), jnp.bfloat16),
            pltpu.VMEM((2, depth, depth), jnp.bfloat16),
            pltpu.VMEM((2, nz, full, ny, lanes), jnp.float32),
            pltpu.VMEM((STEPS, 2, nz, full, ny, lanes), jnp.float32),
            pltpu.VMEM((2, 2 * (full - 2) * ny, depth), jnp.bfloat16),
            pltpu.VMEM(lines, jnp.float32),
            pltpu.VMEM((2, *lines), jnp.float32),
            pltpu.VMEM((2, *lines), jnp.float32),
            pltpu.VMEM(lines, jnp.float32),
            pltpu.SMEM((images,), jnp.int32),
            pltpu.SMEM((images, 4), jnp.float32),
            dma((5,)),
            dma((2, nz)),
            dma((2, nz)),
            dma((2, 2)),
            dma((2, 2, nz)),
            dma((STEPS, 2, 2)),
            dma((STEPS, 2, 2)),
            dma((2, 2, nz)),
            dma((2, 2, nz)),
            dma((2, 2, nz)),
            dma((2, 2, nz)),
            dma((2, nz)),
            dma((2, nz)),
        ],
        compiler_params=pltpu.CompilerParams(
            collective_id=0, has_side_effects=True, vmem_limit_bytes=62 * 1024 * 1024
        ),
    )(species, diffusion, z_inverse, starts, weights)


def solution(mesh):
    images, nx, nz = (mesh.shape[axis] for axis in ("img", "gx", "gz"))

    def body(species, diffusion, z_inverse, starts, weights):
        sizes = (images, nx, nz, *species.shape[2:])
        return local(sizes, species, diffusion, z_inverse, starts, weights)

    return jax.shard_map(
        body,
        mesh=mesh,
        in_specs=(P("img", None, "gx", None, "gz"), P(None, "gx", None, "gz"), P(), P(), P()),
        out_specs=P("img", None, "gx", None, "gz"),
        check_vma=False,
    )
```

```python
import functools

import jax
import jax.numpy as jnp
from jax import lax
from jax.experimental import pallas as pl
from jax.experimental.pallas import tpu as pltpu
from jax.sharding import PartitionSpec as P

STEPS = 4
HALO = 2


step_size = 0.05
MESH = pl.DeviceIdType.MESH
both = (0, 1)


def kernel(
    sizes,
    species_ref,
    diffusion_ref,
    z_ref,
    starts_hbm,
    weights_hbm,
    out_ref,
    z_raw,
    z_high,
    z_low,
    coeffs,
    states,
    lhs,
    evolved,
    near,
    far,
    result,
    starts_ref,
    weights_ref,
    local_sem,
    swap_send,
    swap_recv,
    relay_send,
    relay_recv,
    edge_send,
    edge_recv,
    row_send,
    row_recv,
    near_send,
    near_recv,
    far_send,
    far_recv,
    back_send,
    back_recv,
):
    images, nx, nz, width, ny, lanes = sizes
    rows = width // nz
    image, gx, gz = lax.axis_index("img"), lax.axis_index("gx"), lax.axis_index("gz")
    strip = gx * nz + gz
    strips = nx * nz
    full = rows + 2 * HALO
    trades = tuple(step for step in range(1, STEPS) if step % HALO == 0)

    load_z = pltpu.make_async_copy(z_ref, z_raw, local_sem.at[0])
    load_z.start()
    load_starts = pltpu.make_async_copy(starts_hbm, starts_ref, local_sem.at[3])
    load_starts.start()
    load_weights = pltpu.make_async_copy(weights_hbm, weights_ref, local_sem.at[4])
    load_weights.start()

    barrier = pltpu.get_barrier_semaphore()
    for step in range(1, nz):
        other = lax.rem(gz + step, nz)
        pl.semaphore_signal(barrier, inc=1, device_id={"gz": other}, device_id_type=MESH)

    def greet(condition, where):
        @pl.when(condition)
        def _():
            pl.semaphore_signal(barrier, inc=1, device_id=where, device_id_type=MESH)

    greet(image > 0, {"img": image - 1})
    greet(image < images - 1, {"img": image + 1})
    greet(gx > 0, {"gx": gx - 1, "gz": nz - 1})
    greet(gx < nx - 1, {"gx": gx + 1, "gz": 0})

    @pl.when(gz == 0)
    def _():
        for other in range(nz):
            greet(gx > 0, {"gx": gx - 1, "gz": other})

    @pl.when(gz == nz - 1)
    def _():
        for other in range(nz):
            greet(gx < nx - 1, {"gx": gx + 1, "gz": other})

    def one(condition):
        return jnp.where(condition, 1, 0)

    below, above = one(gx > 0), one(gx < nx - 1)
    expected = (nz - 1) + one(image > 0) + one(image < images - 1) + below + above
    expected = expected + nz * (below * one(gz == 0) + above * one(gz == nz - 1))
    pl.semaphore_wait(barrier, expected)

    sources = (diffusion_ref, species_ref.at[0])
    targets = (coeffs, states.at[0])

    def span(k):
        return max(0, k * rows - HALO), min(width, k * rows + rows + HALO)

    def swap(which, k, sender):
        low, high = span(k)
        first = low - (k * rows - HALO)
        return pltpu.make_async_remote_copy(
            src_ref=sources[which].at[:, low:high],
            dst_ref=targets[which].at[:, sender, first : first + high - low],
            send_sem=swap_send.at[which, k],
            recv_sem=swap_recv.at[which, sender],
            device_id={"gz": k},
            device_id_type=MESH,
        )

    paired = images % 2 == 0 and nz % 2 == 0
    mine = lax.rem(image, 2)

    def crosses(k, sender):
        return paired and k // (nz // 2) != sender // (nz // 2)

    def cross(k, sender):
        low, high = span(k)
        first = low - (k * rows - HALO)
        return pltpu.make_async_remote_copy(
            src_ref=diffusion_ref.at[mine, low:high],
            dst_ref=coeffs.at[mine, sender, first : first + high - low],
            send_sem=swap_send.at[0, k],
            recv_sem=swap_recv.at[0, sender],
            device_id={"gz": k},
            device_id_type=MESH,
        )

    def relay(k, sender, species):
        low, high = span(k)
        first = low - (k * rows - HALO)
        part = coeffs.at[species, sender, first : first + high - low]
        return pltpu.make_async_remote_copy(
            src_ref=part,
            dst_ref=part,
            send_sem=relay_send.at[sender],
            recv_sem=relay_recv.at[sender],
            device_id={"img": image + 1 - 2 * mine},
            device_id_type=MESH,
        )

    def own(which, k):
        low, high = span(k)
        first = low - (k * rows - HALO)
        return pltpu.make_async_copy(
            sources[which].at[:, low:high],
            targets[which].at[:, k, first : first + high - low],
            local_sem.at[1 + which],
        )

    def edge_up(which, sender):
        return pltpu.make_async_remote_copy(
            src_ref=sources[which].at[:, width - HALO : width],
            dst_ref=targets[which].at[:, sender, 0:HALO],
            send_sem=edge_send.at[which, 0],
            recv_sem=edge_recv.at[which, 0, sender],
            device_id={"gx": gx + 1, "gz": 0},
            device_id_type=MESH,
        )

    def edge_down(which, sender):
        return pltpu.make_async_remote_copy(
            src_ref=sources[which].at[:, 0:HALO],
            dst_ref=targets[which].at[:, sender, rows + HALO : full],
            send_sem=edge_send.at[which, 1],
            recv_sem=edge_recv.at[which, 1, sender],
            device_id={"gx": gx - 1, "gz": nz - 1},
            device_id_type=MESH,
        )

    for me in range(nz):

        @pl.when(gz == me)
        def _(me=me):
            for k in range(nz):
                if crosses(k, me):
                    cross(k, me).start()

    for which in (1, 0):
        for me in range(nz):

            @pl.when(gz == me)
            def _(which=which, me=me):
                others = [(me + step) % nz for step in range(1, nz)]
                for k in sorted(others, key=lambda k: not crosses(k, me)):
                    if which == 1 or not crosses(k, me):
                        swap(which, k, me).start()
                own(which, me).start()

        @pl.when(gx < nx - 1)
        def _(which=which):
            edge_up(which, gz).start()

        @pl.when(gx > 0)
        def _(which=which):
            edge_down(which, gz).start()

    @pl.when(strip == 0)
    def _():
        for part in (coeffs, *[states.at[i] for i in (0, *trades)]):
            part[:, :, 0:HALO] = jnp.zeros((2, nz, HALO, ny, lanes), jnp.float32)

    @pl.when(strip == strips - 1)
    def _():
        for part in (coeffs, *[states.at[i] for i in (0, *trades)]):
            part[:, :, rows + HALO : full] = jnp.zeros((2, nz, HALO, ny, lanes), jnp.float32)

    def clear(condition, part):
        @pl.when(condition)
        def _():
            part[...] = jnp.zeros(part.shape, jnp.float32)

    clear(image < 1, near.at[0])
    clear(image > images - 2, near.at[1])
    clear(image < 2, far.at[0])
    clear(image > images - 3, far.at[1])

    load_z.wait()
    for s in both:
        for block in range(nz):
            part = slice(block * lanes, (block + 1) * lanes)
            turned = z_raw[s, part, :].T
            high = turned.astype(jnp.bfloat16)
            z_high[s, :, part] = high
            z_low[s, :, part] = (turned - high.astype(jnp.float32)).astype(jnp.bfloat16)

    for me in range(nz):

        @pl.when(gz == me)
        def _(me=me):
            for sender in range(nz):
                if crosses(me, sender):
                    cross(me, sender).wait_recv()
                    relay(me, sender, mine).start()

    def arrived(which):
        for me in range(nz):

            @pl.when(gz == me)
            def _(me=me):
                own(which, me).wait()
                for sender in range(nz):
                    if which == 0 and crosses(me, sender):
                        relay(me, sender, 1 - mine).wait_recv()
                    elif sender != me:
                        low, high = span(me)
                        first = low - (me * rows - HALO)
                        part = targets[which].at[:, sender, first : first + high - low]
                        pltpu.make_async_copy(part, part, swap_recv.at[which, sender]).wait()

        @pl.when((gz == 0) & (gx > 0))
        def _():
            for sender in range(nz):
                edge_up(which, sender).wait_recv()

        @pl.when((gz == nz - 1) & (gx < nx - 1))
        def _():
            for sender in range(nz):
                edge_down(which, sender).wait_recv()

    def row_up(step, s):
        p = strip + 1
        return pltpu.make_async_remote_copy(
            src_ref=states.at[step, s, :, rows : rows + HALO],
            dst_ref=states.at[step, s, :, 0:HALO],
            send_sem=row_send.at[step, s, 0],
            recv_sem=row_recv.at[step, s, 0],
            device_id={"gx": lax.div(p, nz), "gz": lax.rem(p, nz)},
            device_id_type=MESH,
        )

    def row_down(step, s):
        p = strip - 1 + nz
        return pltpu.make_async_remote_copy(
            src_ref=states.at[step, s, :, HALO : 2 * HALO],
            dst_ref=states.at[step, s, :, rows + HALO : full],
            send_sem=row_send.at[step, s, 1],
            recv_sem=row_recv.at[step, s, 1],
            device_id={"gx": lax.div(p, nz) - 1, "gz": lax.rem(p, nz)},
            device_id_type=MESH,
        )

    arrived(1)
    arrived(0)
    half = 0.5 * step_size

    def to_near(s, g, side):
        return pltpu.make_async_remote_copy(
            src_ref=evolved.at[s, g],
            dst_ref=near.at[side, s, g],
            send_sem=near_send.at[side, s, g],
            recv_sem=near_recv.at[side, s, g],
            device_id={"img": image + 1 - 2 * side},
            device_id_type=MESH,
        )

    def to_far(s, g, side):
        return pltpu.make_async_remote_copy(
            src_ref=near.at[side, s, g],
            dst_ref=far.at[side, s, g],
            send_sem=far_send.at[side, s, g],
            recv_sem=far_recv.at[side, s, g],
            device_id={"img": image + 1 - 2 * side},
            device_id_type=MESH,
        )

    turns = [lax.rem(gz + turn, nz) for turn in range(1, nz)]
    order = [(s, g) for s in both for g in turns] + [(s, gz) for s in both]

    can_send = (image < images - 1, image > 0)
    has_near = (image > 0, image < images - 1)
    has_far = (image > 1, image < images - 2)

    for step in range(STEPS):
        state = states.at[step]
        if step in trades:
            for s in both:

                @pl.when(strip > 0)
                def _(s=s):
                    row_up(step, s).wait_recv()

                @pl.when(strip < strips - 1)
                def _(s=s):
                    row_down(step, s).wait_recv()

        spare = HALO - 1 - step % HALO
        if step == STEPS - 1:
            spare = 0
        count = rows + 2 * spare
        low, cells = HALO - spare, count * ny
        inner = slice(low, low + count)
        outer = slice(low - 1, low + count + 1)
        place = lax.broadcasted_iota(jnp.int32, (count, ny, lanes), 1)
        row = lax.broadcasted_iota(jnp.int32, (count, ny, lanes), 0)
        beyond = (strip == 0) & (row < spare) | (strip == strips - 1) & (row >= rows + spare)
        for g in range(nz):
            first, second = state[0, g, inner], state[1, g, inner]
            reactions = (
                first - first * first * first - second + 0.2,
                0.5 * (first - second),
            )
            for s in both:
                c = state[s, g, outer]
                d = coeffs[s, g, outer]
                across = (d[:-1] + d[1:]) * (c[1:] - c[:-1])
                centre, spread = c[1:-1], d[1:-1]
                last = place == ny - 1
                c_next = jnp.where(last, 0.0, pltpu.roll(centre, ny - 1, 1))
                d_next = jnp.where(last, 0.0, pltpu.roll(spread, ny - 1, 1))
                along = (spread + d_next) * (c_next - centre)
                before = jnp.where(place == 0, spread * centre, pltpu.roll(along, 1, 1))
                flux = (across[1:] - across[:-1]) + (along - before)
                source = centre + step_size * reactions[s] + half * flux
                if spare > 0:
                    source = jnp.where(beyond, 0.0, source)
                source = source.reshape(cells, lanes)
                high = source.astype(jnp.bfloat16)
                part = slice(g * lanes, (g + 1) * lanes)
                lhs[s, 0:cells, part] = high
                lhs[s, cells : 2 * cells, part] = (source - high.astype(jnp.float32)).astype(jnp.bfloat16)

        for s in both:
            product = jnp.dot(lhs[s], z_high[s], preferred_element_type=jnp.float32)
            small = jnp.dot(lhs[s, 0:cells], z_low[s], preferred_element_type=jnp.float32)
            solved = product[0:cells] + (product[cells : 2 * cells] + small)
            for g in range(nz):
                block = solved[:, g * lanes : (g + 1) * lanes].reshape(count, ny, lanes)
                if step < STEPS - 1:
                    states[step + 1, s, g, inner] = block
                else:
                    evolved[s, g] = block
            if step + 1 in trades:

                @pl.when(strip < strips - 1)
                def _(s=s, step=step):
                    row_up(step + 1, s).start()

                @pl.when(strip > 0)
                def _(s=s, step=step):
                    row_down(step + 1, s).start()

            elif step == STEPS - 1:
                ready = order[: nz - 1] if s == 0 else order[nz - 1 :]
                for t, g in ready:
                    for side in both:

                        @pl.when(can_send[side])
                        def _(t=t, g=g, side=side):
                            to_near(t, g, side).start()

    for s, g in order:
        for side in both:

            @pl.when(has_near[side])
            def _(s=s, g=g, side=side):
                to_near(s, g, side).wait_recv()

                @pl.when(can_send[side])
                def _():
                    to_far(s, g, side).start()

    load_starts.wait()
    load_weights.wait()
    start = starts_ref[image]

    def coef(offset):
        total = jnp.float32(0.0)
        for k in range(4):
            total = total + jnp.where(start + k == image + offset, weights_ref[image, k], 0.0)
        return total

    coefs = [coef(offset) for offset in range(-2, 3)]

    def back(s, g, sender):
        return pltpu.make_async_remote_copy(
            src_ref=result.at[s, g],
            dst_ref=out_ref.at[0, s, pl.ds(sender * rows, rows)],
            send_sem=back_send.at[s, g],
            recv_sem=back_recv.at[s, sender],
            device_id={"gz": g},
            device_id_type=MESH,
        )

    def keep(s, g):
        return pltpu.make_async_copy(
            result.at[s, g], out_ref.at[0, s, pl.ds(gz * rows, rows)], back_send.at[s, g]
        )

    for turn, (s, g) in enumerate(order):
        for side in both:

            @pl.when(has_far[side])
            def _(s=s, g=g, side=side):
                to_far(s, g, side).wait_recv()

        total = coefs[0] * far[0, s, g] + coefs[1] * near[0, s, g]
        total = total + coefs[2] * evolved[s, g]
        total = total + coefs[3] * near[1, s, g] + coefs[4] * far[1, s, g]
        result[s, g] = total
        if turn < len(order) - 2:
            back(s, g, gz).start()
        else:
            keep(s, g).start()

    for which in both:
        for me in range(nz):

            @pl.when(gz == me)
            def _(which=which, me=me):
                for k in range(nz):
                    if which == 0 and crosses(k, me):
                        cross(k, me).wait_send()
                        relay(me, k, mine).wait_send()
                    elif k != me:
                        swap(which, k, me).wait_send()

        @pl.when(gx < nx - 1)
        def _(which=which):
            edge_up(which, gz).wait_send()

        @pl.when(gx > 0)
        def _(which=which):
            edge_down(which, gz).wait_send()

    for step in trades:
        for s in both:

            @pl.when(strip < strips - 1)
            def _(s=s, step=step):
                row_up(step, s).wait_send()

            @pl.when(strip > 0)
            def _(s=s, step=step):
                row_down(step, s).wait_send()

    for s in both:
        for g in range(nz):
            for side in both:

                @pl.when(can_send[side])
                def _(s=s, g=g, side=side):
                    to_near(s, g, side).wait_send()

                @pl.when(can_send[side] & has_near[side])
                def _(s=s, g=g, side=side):
                    to_far(s, g, side).wait_send()

            @pl.when(gz != g)
            def _(s=s, g=g):
                back(s, g, gz).wait_send()
                back(s, g, g).wait_recv()

            @pl.when(gz == g)
            def _(s=s, g=g):
                keep(s, g).wait()


def local(sizes, species, diffusion, z_inverse, starts, weights):
    images, nx, nz, width, ny, lanes = sizes
    rows = width // nz
    depth = nz * lanes
    full = rows + 2 * HALO
    dma = pltpu.SemaphoreType.DMA
    anywhere = pl.BlockSpec(memory_space=pl.ANY)
    lines = (2, nz, rows, ny, lanes)
    operands = (species, diffusion, z_inverse, starts, weights)
    operands = [pltpu.with_memory_space_constraint(each, pltpu.HBM) for each in operands]
    return pl.pallas_call(
        functools.partial(kernel, sizes),
        out_shape=jax.ShapeDtypeStruct(species.shape, jnp.float32),
        in_specs=[anywhere] * 5,
        out_specs=anywhere,
        scratch_shapes=[
            pltpu.VMEM((2, depth, depth), jnp.float32),
            pltpu.VMEM((2, depth, depth), jnp.bfloat16),
            pltpu.VMEM((2, depth, depth), jnp.bfloat16),
            pltpu.VMEM((2, nz, full, ny, lanes), jnp.float32),
            pltpu.VMEM((STEPS, 2, nz, full, ny, lanes), jnp.float32),
            pltpu.VMEM((2, 2 * (full - 2) * ny, depth), jnp.bfloat16),
            pltpu.VMEM(lines, jnp.float32),
            pltpu.VMEM((2, *lines), jnp.float32),
            pltpu.VMEM((2, *lines), jnp.float32),
            pltpu.VMEM(lines, jnp.float32),
            pltpu.SMEM((images,), jnp.int32),
            pltpu.SMEM((images, 4), jnp.float32),
            dma((5,)),
            dma((2, nz)),
            dma((2, nz)),
            dma((nz,)),
            dma((nz,)),
            dma((2, 2)),
            dma((2, 2, nz)),
            dma((STEPS, 2, 2)),
            dma((STEPS, 2, 2)),
            dma((2, 2, nz)),
            dma((2, 2, nz)),
            dma((2, 2, nz)),
            dma((2, 2, nz)),
            dma((2, nz)),
            dma((2, nz)),
        ],
        compiler_params=pltpu.CompilerParams(
            collective_id=0, has_side_effects=True, vmem_limit_bytes=40 * 1024 * 1024
        ),
    )(*operands)


def solution(mesh):
    images, nx, nz = (mesh.shape[axis] for axis in ("img", "gx", "gz"))

    def body(species, diffusion, z_inverse, starts, weights):
        sizes = (images, nx, nz, *species.shape[2:])
        return local(sizes, species, diffusion, z_inverse, starts, weights)

    return jax.shard_map(
        body,
        mesh=mesh,
        in_specs=(P("img", None, "gx", None, "gz"), P(None, "gx", None, "gz"), P(), P(), P()),
        out_specs=P("img", None, "gx", None, "gz"),
        check_vma=False,
    )
```

```python
import functools

import jax
import jax.numpy as jnp
from jax import lax
from jax.experimental import pallas as pl
from jax.experimental.pallas import tpu as pltpu
from jax.sharding import PartitionSpec as P

STEPS = 4
HALO = 2


step_size = 0.05
MESH = pl.DeviceIdType.MESH
both = (0, 1)


def kernel(
    sizes,
    species_ref,
    diffusion_ref,
    z_ref,
    starts_hbm,
    weights_hbm,
    out_ref,
    z_raw,
    z_high,
    z_low,
    coeffs,
    states,
    lhs,
    evolved,
    near,
    far,
    result,
    starts_ref,
    weights_ref,
    local_sem,
    swap_send,
    swap_recv,
    relay_send,
    relay_recv,
    edge_send,
    edge_recv,
    row_send,
    row_recv,
    near_send,
    near_recv,
    far_send,
    far_recv,
    back_send,
    back_recv,
):
    images, nx, nz, width, ny, lanes = sizes
    rows = width // nz
    image, gx, gz = lax.axis_index("img"), lax.axis_index("gx"), lax.axis_index("gz")
    strip = gx * nz + gz
    strips = nx * nz
    full = rows + 2 * HALO
    trades = tuple(step for step in range(1, STEPS) if step % HALO == 0)

    load_z = pltpu.make_async_copy(z_ref, z_raw, local_sem.at[0])
    load_z.start()
    load_starts = pltpu.make_async_copy(starts_hbm, starts_ref, local_sem.at[3])
    load_starts.start()
    load_weights = pltpu.make_async_copy(weights_hbm, weights_ref, local_sem.at[4])
    load_weights.start()

    barrier = pltpu.get_barrier_semaphore()
    for step in range(1, nz):
        other = lax.rem(gz + step, nz)
        pl.semaphore_signal(barrier, inc=1, device_id={"gz": other}, device_id_type=MESH)

    def greet(condition, where):
        @pl.when(condition)
        def _():
            pl.semaphore_signal(barrier, inc=1, device_id=where, device_id_type=MESH)

    greet(image > 0, {"img": image - 1})
    greet(image < images - 1, {"img": image + 1})
    greet(gx > 0, {"gx": gx - 1, "gz": nz - 1})
    greet(gx < nx - 1, {"gx": gx + 1, "gz": 0})

    @pl.when(gz == 0)
    def _():
        for other in range(nz):
            greet(gx > 0, {"gx": gx - 1, "gz": other})

    @pl.when(gz == nz - 1)
    def _():
        for other in range(nz):
            greet(gx < nx - 1, {"gx": gx + 1, "gz": other})

    def one(condition):
        return jnp.where(condition, 1, 0)

    below, above = one(gx > 0), one(gx < nx - 1)
    expected = (nz - 1) + one(image > 0) + one(image < images - 1) + below + above
    expected = expected + nz * (below * one(gz == 0) + above * one(gz == nz - 1))
    pl.semaphore_wait(barrier, expected)

    sources = (diffusion_ref, species_ref.at[0])
    targets = (coeffs, states.at[0])

    def span(k):
        return max(0, k * rows - HALO), min(width, k * rows + rows + HALO)

    def swap(which, k, sender):
        low, high = span(k)
        first = low - (k * rows - HALO)
        return pltpu.make_async_remote_copy(
            src_ref=sources[which].at[:, low:high],
            dst_ref=targets[which].at[:, sender, first : first + high - low],
            send_sem=swap_send.at[which, k],
            recv_sem=swap_recv.at[which, sender],
            device_id={"gz": k},
            device_id_type=MESH,
        )

    paired = images % 2 == 0 and nz % 2 == 0
    mine = lax.rem(image, 2)

    def crosses(k, sender):
        return paired and k // (nz // 2) != sender // (nz // 2)

    def cross(k, sender):
        low, high = span(k)
        first = low - (k * rows - HALO)
        return pltpu.make_async_remote_copy(
            src_ref=diffusion_ref.at[mine, low:high],
            dst_ref=coeffs.at[mine, sender, first : first + high - low],
            send_sem=swap_send.at[0, k],
            recv_sem=swap_recv.at[0, sender],
            device_id={"gz": k},
            device_id_type=MESH,
        )

    def relay(k, sender, species):
        low, high = span(k)
        first = low - (k * rows - HALO)
        part = coeffs.at[species, sender, first : first + high - low]
        return pltpu.make_async_remote_copy(
            src_ref=part,
            dst_ref=part,
            send_sem=relay_send.at[sender],
            recv_sem=relay_recv.at[sender],
            device_id={"img": image + 1 - 2 * mine},
            device_id_type=MESH,
        )

    def own(which, k):
        low, high = span(k)
        first = low - (k * rows - HALO)
        return pltpu.make_async_copy(
            sources[which].at[:, low:high],
            targets[which].at[:, k, first : first + high - low],
            local_sem.at[1 + which],
        )

    def edge_up(which, sender):
        return pltpu.make_async_remote_copy(
            src_ref=sources[which].at[:, width - HALO : width],
            dst_ref=targets[which].at[:, sender, 0:HALO],
            send_sem=edge_send.at[which, 0],
            recv_sem=edge_recv.at[which, 0, sender],
            device_id={"gx": gx + 1, "gz": 0},
            device_id_type=MESH,
        )

    def edge_down(which, sender):
        return pltpu.make_async_remote_copy(
            src_ref=sources[which].at[:, 0:HALO],
            dst_ref=targets[which].at[:, sender, rows + HALO : full],
            send_sem=edge_send.at[which, 1],
            recv_sem=edge_recv.at[which, 1, sender],
            device_id={"gx": gx - 1, "gz": nz - 1},
            device_id_type=MESH,
        )

    for which in (1, 0):

        @pl.when(gx < nx - 1)
        def _(which=which):
            edge_up(which, gz).start()

        @pl.when(gx > 0)
        def _(which=which):
            edge_down(which, gz).start()

    for me in range(nz):

        @pl.when(gz == me)
        def _(me=me):
            for k in range(nz):
                if crosses(k, me):
                    cross(k, me).start()

    for which in (1, 0):
        for me in range(nz):

            @pl.when(gz == me)
            def _(which=which, me=me):
                others = [(me + step) % nz for step in range(1, nz)]
                for k in sorted(others, key=lambda k: not crosses(k, me)):
                    if which == 1 or not crosses(k, me):
                        swap(which, k, me).start()
                own(which, me).start()

    @pl.when(strip == 0)
    def _():
        for part in (coeffs, *[states.at[i] for i in (0, *trades)]):
            part[:, :, 0:HALO] = jnp.zeros((2, nz, HALO, ny, lanes), jnp.float32)

    @pl.when(strip == strips - 1)
    def _():
        for part in (coeffs, *[states.at[i] for i in (0, *trades)]):
            part[:, :, rows + HALO : full] = jnp.zeros((2, nz, HALO, ny, lanes), jnp.float32)

    def clear(condition, part):
        @pl.when(condition)
        def _():
            part[...] = jnp.zeros(part.shape, jnp.float32)

    clear(image < 1, near.at[0])
    clear(image > images - 2, near.at[1])
    clear(image < 2, far.at[0])
    clear(image > images - 3, far.at[1])

    load_z.wait()
    for s in both:
        for block in range(nz):
            part = slice(block * lanes, (block + 1) * lanes)
            turned = z_raw[s, part, :].T
            high = turned.astype(jnp.bfloat16)
            z_high[s, :, part] = high
            z_low[s, :, part] = (turned - high.astype(jnp.float32)).astype(jnp.bfloat16)

    for me in range(nz):

        @pl.when(gz == me)
        def _(me=me):
            for sender in range(nz):
                if crosses(me, sender):
                    cross(me, sender).wait_recv()
                    relay(me, sender, mine).start()

    def arrived(which):
        for me in range(nz):

            @pl.when(gz == me)
            def _(me=me):
                own(which, me).wait()
                for sender in range(nz):
                    if which == 0 and crosses(me, sender):
                        relay(me, sender, 1 - mine).wait_recv()
                    elif sender != me:
                        low, high = span(me)
                        first = low - (me * rows - HALO)
                        part = targets[which].at[:, sender, first : first + high - low]
                        pltpu.make_async_copy(part, part, swap_recv.at[which, sender]).wait()

        @pl.when((gz == 0) & (gx > 0))
        def _():
            for sender in range(nz):
                edge_up(which, sender).wait_recv()

        @pl.when((gz == nz - 1) & (gx < nx - 1))
        def _():
            for sender in range(nz):
                edge_down(which, sender).wait_recv()

    def row_up(step, s):
        p = strip + 1
        return pltpu.make_async_remote_copy(
            src_ref=states.at[step, s, :, rows : rows + HALO],
            dst_ref=states.at[step, s, :, 0:HALO],
            send_sem=row_send.at[step, s, 0],
            recv_sem=row_recv.at[step, s, 0],
            device_id={"gx": lax.div(p, nz), "gz": lax.rem(p, nz)},
            device_id_type=MESH,
        )

    def row_down(step, s):
        p = strip - 1 + nz
        return pltpu.make_async_remote_copy(
            src_ref=states.at[step, s, :, HALO : 2 * HALO],
            dst_ref=states.at[step, s, :, rows + HALO : full],
            send_sem=row_send.at[step, s, 1],
            recv_sem=row_recv.at[step, s, 1],
            device_id={"gx": lax.div(p, nz) - 1, "gz": lax.rem(p, nz)},
            device_id_type=MESH,
        )

    arrived(1)
    arrived(0)
    half = 0.5 * step_size

    def to_near(s, g, side):
        return pltpu.make_async_remote_copy(
            src_ref=evolved.at[s, g],
            dst_ref=near.at[side, s, g],
            send_sem=near_send.at[side, s, g],
            recv_sem=near_recv.at[side, s, g],
            device_id={"img": image + 1 - 2 * side},
            device_id_type=MESH,
        )

    def to_far(s, g, side):
        return pltpu.make_async_remote_copy(
            src_ref=near.at[side, s, g],
            dst_ref=far.at[side, s, g],
            send_sem=far_send.at[side, s, g],
            recv_sem=far_recv.at[side, s, g],
            device_id={"img": image + 1 - 2 * side},
            device_id_type=MESH,
        )

    turns = [lax.rem(gz + turn, nz) for turn in range(1, nz)]
    order = [(s, g) for s in both for g in turns] + [(s, gz) for s in both]

    can_send = (image < images - 1, image > 0)
    has_near = (image > 0, image < images - 1)
    has_far = (image > 1, image < images - 2)

    for step in range(STEPS):
        state = states.at[step]
        if step in trades:
            for s in both:

                @pl.when(strip > 0)
                def _(s=s):
                    row_up(step, s).wait_recv()

                @pl.when(strip < strips - 1)
                def _(s=s):
                    row_down(step, s).wait_recv()

        spare = HALO - 1 - step % HALO
        if step == STEPS - 1:
            spare = 0
        count = rows + 2 * spare
        low, cells = HALO - spare, count * ny
        inner = slice(low, low + count)
        outer = slice(low - 1, low + count + 1)
        place = lax.broadcasted_iota(jnp.int32, (count, ny, lanes), 1)
        row = lax.broadcasted_iota(jnp.int32, (count, ny, lanes), 0)
        beyond = (strip == 0) & (row < spare) | (strip == strips - 1) & (row >= rows + spare)
        for g in range(nz):
            first, second = state[0, g, inner], state[1, g, inner]
            reactions = (
                first - first * first * first - second + 0.2,
                0.5 * (first - second),
            )
            for s in both:
                c = state[s, g, outer]
                d = coeffs[s, g, outer]
                across = (d[:-1] + d[1:]) * (c[1:] - c[:-1])
                centre, spread = c[1:-1], d[1:-1]
                last = place == ny - 1
                c_next = jnp.where(last, 0.0, pltpu.roll(centre, ny - 1, 1))
                d_next = jnp.where(last, 0.0, pltpu.roll(spread, ny - 1, 1))
                along = (spread + d_next) * (c_next - centre)
                before = jnp.where(place == 0, spread * centre, pltpu.roll(along, 1, 1))
                flux = (across[1:] - across[:-1]) + (along - before)
                source = centre + step_size * reactions[s] + half * flux
                if spare > 0:
                    source = jnp.where(beyond, 0.0, source)
                source = source.reshape(cells, lanes)
                high = source.astype(jnp.bfloat16)
                part = slice(g * lanes, (g + 1) * lanes)
                lhs[s, 0:cells, part] = high
                lhs[s, cells : 2 * cells, part] = (source - high.astype(jnp.float32)).astype(jnp.bfloat16)

        for s in both:
            product = jnp.dot(lhs[s], z_high[s], preferred_element_type=jnp.float32)
            small = jnp.dot(lhs[s, 0:cells], z_low[s], preferred_element_type=jnp.float32)
            solved = product[0:cells] + (product[cells : 2 * cells] + small)
            for g in range(nz):
                block = solved[:, g * lanes : (g + 1) * lanes].reshape(count, ny, lanes)
                if step < STEPS - 1:
                    states[step + 1, s, g, inner] = block
                else:
                    evolved[s, g] = block
            if step + 1 in trades:

                @pl.when(strip < strips - 1)
                def _(s=s, step=step):
                    row_up(step + 1, s).start()

                @pl.when(strip > 0)
                def _(s=s, step=step):
                    row_down(step + 1, s).start()

            elif step == STEPS - 1:
                ready = order[: nz - 1] if s == 0 else order[nz - 1 :]
                for t, g in ready:
                    for side in both:

                        @pl.when(can_send[side])
                        def _(t=t, g=g, side=side):
                            to_near(t, g, side).start()

    for s, g in order:
        for side in both:

            @pl.when(has_near[side])
            def _(s=s, g=g, side=side):
                to_near(s, g, side).wait_recv()

                @pl.when(can_send[side])
                def _():
                    to_far(s, g, side).start()

    load_starts.wait()
    load_weights.wait()
    start = starts_ref[image]

    def coef(offset):
        total = jnp.float32(0.0)
        for k in range(4):
            total = total + jnp.where(start + k == image + offset, weights_ref[image, k], 0.0)
        return total

    coefs = [coef(offset) for offset in range(-2, 3)]

    def back(s, g, sender):
        return pltpu.make_async_remote_copy(
            src_ref=result.at[s, g],
            dst_ref=out_ref.at[0, s, pl.ds(sender * rows, rows)],
            send_sem=back_send.at[s, g],
            recv_sem=back_recv.at[s, sender],
            device_id={"gz": g},
            device_id_type=MESH,
        )

    def keep(s, g):
        return pltpu.make_async_copy(
            result.at[s, g], out_ref.at[0, s, pl.ds(gz * rows, rows)], back_send.at[s, g]
        )

    for turn, (s, g) in enumerate(order):
        for side in both:

            @pl.when(has_far[side])
            def _(s=s, g=g, side=side):
                to_far(s, g, side).wait_recv()

        total = coefs[0] * far[0, s, g] + coefs[1] * near[0, s, g]
        total = total + coefs[2] * evolved[s, g]
        total = total + coefs[3] * near[1, s, g] + coefs[4] * far[1, s, g]
        result[s, g] = total
        if turn < len(order) - 2:
            back(s, g, gz).start()
        else:
            keep(s, g).start()

    for which in both:
        for me in range(nz):

            @pl.when(gz == me)
            def _(which=which, me=me):
                for k in range(nz):
                    if which == 0 and crosses(k, me):
                        cross(k, me).wait_send()
                        relay(me, k, mine).wait_send()
                    elif k != me:
                        swap(which, k, me).wait_send()

        @pl.when(gx < nx - 1)
        def _(which=which):
            edge_up(which, gz).wait_send()

        @pl.when(gx > 0)
        def _(which=which):
            edge_down(which, gz).wait_send()

    for step in trades:
        for s in both:

            @pl.when(strip < strips - 1)
            def _(s=s, step=step):
                row_up(step, s).wait_send()

            @pl.when(strip > 0)
            def _(s=s, step=step):
                row_down(step, s).wait_send()

    for s in both:
        for g in range(nz):
            for side in both:

                @pl.when(can_send[side])
                def _(s=s, g=g, side=side):
                    to_near(s, g, side).wait_send()

                @pl.when(can_send[side] & has_near[side])
                def _(s=s, g=g, side=side):
                    to_far(s, g, side).wait_send()

            @pl.when(gz != g)
            def _(s=s, g=g):
                back(s, g, gz).wait_send()
                back(s, g, g).wait_recv()

            @pl.when(gz == g)
            def _(s=s, g=g):
                keep(s, g).wait()


def local(sizes, species, diffusion, z_inverse, starts, weights):
    images, nx, nz, width, ny, lanes = sizes
    rows = width // nz
    depth = nz * lanes
    full = rows + 2 * HALO
    dma = pltpu.SemaphoreType.DMA
    anywhere = pl.BlockSpec(memory_space=pl.ANY)
    lines = (2, nz, rows, ny, lanes)
    operands = (species, diffusion, z_inverse, starts, weights)
    operands = [pltpu.with_memory_space_constraint(each, pltpu.HBM) for each in operands]
    return pl.pallas_call(
        functools.partial(kernel, sizes),
        out_shape=jax.ShapeDtypeStruct(species.shape, jnp.float32),
        in_specs=[anywhere] * 5,
        out_specs=anywhere,
        scratch_shapes=[
            pltpu.VMEM((2, depth, depth), jnp.float32),
            pltpu.VMEM((2, depth, depth), jnp.bfloat16),
            pltpu.VMEM((2, depth, depth), jnp.bfloat16),
            pltpu.VMEM((2, nz, full, ny, lanes), jnp.float32),
            pltpu.VMEM((STEPS, 2, nz, full, ny, lanes), jnp.float32),
            pltpu.VMEM((2, 2 * (full - 2) * ny, depth), jnp.bfloat16),
            pltpu.VMEM(lines, jnp.float32),
            pltpu.VMEM((2, *lines), jnp.float32),
            pltpu.VMEM((2, *lines), jnp.float32),
            pltpu.VMEM(lines, jnp.float32),
            pltpu.SMEM((images,), jnp.int32),
            pltpu.SMEM((images, 4), jnp.float32),
            dma((5,)),
            dma((2, nz)),
            dma((2, nz)),
            dma((nz,)),
            dma((nz,)),
            dma((2, 2)),
            dma((2, 2, nz)),
            dma((STEPS, 2, 2)),
            dma((STEPS, 2, 2)),
            dma((2, 2, nz)),
            dma((2, 2, nz)),
            dma((2, 2, nz)),
            dma((2, 2, nz)),
            dma((2, nz)),
            dma((2, nz)),
        ],
        compiler_params=pltpu.CompilerParams(
            collective_id=0, has_side_effects=True, vmem_limit_bytes=40 * 1024 * 1024
        ),
    )(*operands)


def solution(mesh):
    images, nx, nz = (mesh.shape[axis] for axis in ("img", "gx", "gz"))

    def body(species, diffusion, z_inverse, starts, weights):
        sizes = (images, nx, nz, *species.shape[2:])
        return local(sizes, species, diffusion, z_inverse, starts, weights)

    return jax.shard_map(
        body,
        mesh=mesh,
        in_specs=(P("img", None, "gx", None, "gz"), P(None, "gx", None, "gz"), P(), P(), P()),
        out_specs=P("img", None, "gx", None, "gz"),
        check_vma=False,
    )
```
